256 devices in a mesh: view: 2 (over core), row: 16 (over x, y), feat: 8 (over z).
Axes of the slice: x: 4, y: 4, z: 8, core: 2. Of those that a mesh axis runs over, the one named last changes fastest.
Arguments:
- views: bfloat16 [2, 98304, 4096], P('view', ('row', 'feat')), may hold values from -8 to 8
- weights: float32 [2, 4096, 256], P('view', ('row', 'feat')), may hold values from -6 to 6
Outputs:
- new_weights: float32 [2, 4096, 256], P('view', ('row', 'feat'))
- projected: bfloat16 [2, 98304, 256], P('view', ('row', 'feat'))
The draws below stay inside these ranges and needn't reach their ends.
All inputs are finite; a program needn't handle non-finite values.
Results may differ from the reference program's by a relative error of at most 0.012.
Values may be sent and summed in bfloat16 or wider, within the bound.
A program may use at most 64 MiB of HBM per device.

```python
import math
import jax
import jax.numpy as jnp
from jax import lax

D = 4096
K = 256
ITERS = 2
ROWS_DEV = 768
N = 98304


def draw_views(key, part):
    key = jax.random.fold_in(key, 11)
    keys = jax.random.split(key, 9)
    band_high = 0.5 * math.pi
    spread = 0.7
    noise = jax.random.normal(keys[7], (2, N, D), jnp.float32)
    omega = band_high * jax.random.uniform(keys[2], (N, 2), jnp.float32)
    phase = jax.random.uniform(keys[3], (N, 2), jnp.float32, -math.pi, math.pi)
    gains = jax.random.normal(keys[4], (N, 2), jnp.float32)
    block_amp = jnp.exp(jax.random.uniform(keys[5], (N // ROWS_DEV,), jnp.float32, -spread, spread))
    row_amp = jnp.repeat(block_amp, ROWS_DEV)
    feat_scale = jnp.exp(jax.random.uniform(keys[6], (2, D), jnp.float32, math.log(0.5), math.log(2.0)))
    stacked = []
    for view_index in range(2):
        placing = jax.random.permutation(keys[view_index], D).astype(jnp.float32)
        latent = gains[:, 0:1] * jnp.cos(omega[:, 0:1] * placing[None, :] + phase[:, 0:1])
        latent = latent + gains[:, 1:2] * jnp.cos(omega[:, 1:2] * placing[None, :] + phase[:, 1:2])
        single = feat_scale[view_index][None, :] * (row_amp[:, None] * latent + 0.5 * noise[view_index])
        stacked.append(jnp.clip(single, -8.0, 8.0))
    return jnp.stack(stacked).astype(jnp.bfloat16)


def level_of(own_key, extent, pieces, least, high):
    def one(position, parts):
        draws = jax.random.uniform(jax.random.fold_in(jax.random.fold_in(own_key, 6), position), (parts,), jnp.float32, least / len(pieces), high / len(pieces))
        return jnp.repeat(jnp.exp(draws), extent[position] // parts).reshape((-1,) + (1,) * (len(extent) - position - 1))

    gain = one(*pieces[0])
    for cut in pieces[1:]:
        gain = gain * one(*cut)
    return gain


def centred(own_key, dims, width, bound, pieces=(), kind=jnp.bfloat16):
    level = level_of(own_key, dims, pieces, -0.22, 0.18) if pieces else 1.0
    values = jax.random.normal(own_key, dims, jnp.float32) * width * level
    return jnp.minimum(jnp.maximum(values, -bound), bound).astype(kind)


def setup_inputs(seed: int = 0) -> dict:
    key_of = jax.random.split(jax.random.key(seed), 3)
    return {
        "views": draw_views(jax.random.fold_in(key_of[2], 71), 0),
        "weights": centred(key_of[1], (2, D, K), 1.0, 6.0, ((0, 2), (1, 128)), jnp.float32),
    }


epsilon = 1e-06
step_rate = 0.5

def reference(views, weights):
    iterate = [weights[0], weights[1]]
    projected = []
    for sweep in range(ITERS):
        scaling = []
        projected = []
        for view_index in range(2):
            summed_proj = jnp.dot(views[view_index], iterate[view_index].astype(jnp.bfloat16), preferred_element_type=jnp.float32)
            col_scale = lax.rsqrt(lax.optimization_barrier(jnp.mean(summed_proj * summed_proj, axis=0)) + epsilon)
            scaling.append(col_scale)
            projected.append((summed_proj * col_scale).astype(jnp.bfloat16))
        updated = []
        for view_index in range(2):
            residue = (projected[view_index].astype(jnp.float32) - projected[1 - view_index].astype(jnp.float32)).astype(jnp.bfloat16)
            grad_total = lax.dot_general(views[view_index], residue, (((0,), (0,)), ((), ())), preferred_element_type=jnp.float32) / N
            updated.append(math.sqrt(D) * (iterate[view_index] * scaling[view_index] - step_rate * grad_total))
        iterate = updated
    return (jnp.stack(iterate), jnp.stack(projected))
```

```python
import functools
import math

import jax
import jax.numpy as jnp
from jax import lax
from jax.experimental import pallas as pl
from jax.experimental.pallas import tpu as pltpu
from jax.sharding import PartitionSpec as P

ITERS = 2
EPSILON = 1e-06
STEP_RATE = 0.5
LANES = 256
PIECE = 16
MESH = pl.DeviceIdType.MESH


def layout(n, nz):
    sizes = {
        "gz": 2 * nz,
        "gm": 4 * n,
        "gl": 4 * n * n,
        "n1": n * n,
        "n2": 2 * nz,
        "swap": 1,
        "r1": 4 * n * n,
        "r2": 4 * n,
        "r3": nz,
    }
    start, places = 0, {}
    for name, count in sizes.items():
        places[name] = start
        start += count
    return places, start


def ring_order(nz):
    return sorted(range(nz), key=lambda d: (min(d, nz - d), d))


def kernel(dims, total_rows, root, x_hbm, w_hbm, wout_ref, proj_ref, *scratch):
    n, nz = dims
    (xs, w_in, perm, xp, xt, wg, pf, pp, rr, n1, n2, gs, r1, t2, r2, t3, r3,
     own_w, send_sem, recv_sem, load_sem) = scratch
    rows, feats = xs.shape
    blocks = own_w.shape[0]
    near = nz // 2
    offs = ring_order(nz)
    places, _ = layout(n, nz)
    strip = nz * 2 * PIECE
    span = near * PIECE
    others = sorted(range(1, n), key=lambda d: (min(d, n - d), d))
    by_m = others + [0]

    v = lax.axis_index("view")
    r = lax.axis_index("row")
    z = lax.axis_index("feat")
    x, y = r // n, lax.rem(r, n)

    def ahead(i, d, size):
        return lax.rem(i + d, size) if d else i

    def device(dv, dx, dy, dz):
        return (ahead(v, dv, 2), ahead(x, dx, n) * n + ahead(y, dy, n), ahead(z, dz, nz))

    def along_l(p, d):
        return (0, d, 0, 0) if p == 0 else (0, 0, d, 0)

    def along_m(p, d):
        return (0, 0, d, 0) if p == 0 else (0, d, 0, 0)

    partners = [(0, dx, dy, 0) for dx in range(n) for dy in range(n) if dx or dy]
    partners += [(dv, 0, 0, dz) for dv in range(2) for dz in range(nz) if dv or dz]

    load_w = pltpu.make_async_copy(w_hbm, w_in, load_sem.at[1])
    load_w.start()
    load_x = pltpu.make_async_copy(x_hbm, xs, load_sem.at[0])
    load_x.start()
    barrier = pltpu.get_barrier_semaphore()
    for to in partners:
        pl.semaphore_signal(barrier, inc=1, device_id=device(*to), device_id_type=MESH)

    pending = []
    flying = {}

    def send(s, h, name, index, src, dst, to):
        where = places[name] + index
        copy = pltpu.make_async_remote_copy(
            src_ref=src,
            dst_ref=dst,
            send_sem=send_sem.at[s, h, where],
            recv_sem=recv_sem.at[s, h, where],
            device_id=device(*to),
            device_id_type=MESH,
        )
        copy.start()
        flying[s, h, name, index] = copy

    def arrive(s, h, name, index):
        copy = flying.pop((s, h, name, index))
        copy.wait_recv()
        pending.append(copy)

    def drain(keep):
        while len(pending) > keep:
            pending.pop(0).wait_send()

    def gather_z(s, h):
        for slot in reversed(range(1, nz)):
            for p in range(2):
                send(s, h, "gz", slot * 2 + p, wg.at[s, h, p, 0, 0, 0, 0],
                     wg.at[s, h, p, slot // near, 0, 0, slot % near], (0, 0, 0, (nz - offs[slot]) % nz))

    def gather_m(g, s, h):
        for slot in range(g * near, (g + 1) * near):
            for p in range(2):
                if slot:
                    arrive(s, h, "gz", slot * 2 + p)
        for p in range(2):
            src = wg.at[s, h, p, g, 0, 0]
            for e in others:
                send(s, h, "gm", (p * 2 + g) * n + e, src, wg.at[s, h, p, g, 0, e], along_m(p, n - e))
        for p in range(2):
            src = wg.at[s, h, p, g, 0, 0]
            for d in others:
                send(s, h, "gl", ((p * 2 + g) * n + d) * n, src, wg.at[s, h, p, g, d, 0], along_l(p, n - d))

    def gather_l(g, s, h):
        for e in others:
            for p in range(2):
                arrive(s, h, "gm", (p * 2 + g) * n + e)
                src = wg.at[s, h, p, g, 0, e]
                for d in others:
                    send(s, h, "gl", ((p * 2 + g) * n + d) * n + e, src, wg.at[s, h, p, g, d, e], along_l(p, n - d))

    def project(g, s, h):
        for d in [0] + others:
            for p in range(2):
                if d:
                    for e in range(n):
                        arrive(s, h, "gl", ((p * 2 + g) * n + d) * n + e)
                width = n * span
                part = jnp.dot(
                    xp[p, g, :, d * width:(d + 1) * width],
                    wg[s, h, p, g, d].reshape(width, LANES),
                    preferred_element_type=jnp.float32,
                )
                if g or d or p:
                    part += pf[s, h]
                pf[s, h] = part
        if g:
            part = pf[s, h]
            n1[s, h, 0] = jnp.sum(part * part, axis=0, keepdims=True)
            for dx in range(n):
                for dy in range(n):
                    if dx or dy:
                        to = dx * n + dy
                        send(s, h, "n1", to, n1.at[s, h, 0], n1.at[s, h, to], (0, dx, dy, 0))
            send(s, h, "swap", 0, pf.at[s, h], pp.at[s, h], (1, 0, 0, 0))

    def norm_2(s, h):
        for to in range(1, n * n):
            arrive(s, h, "n1", to)
        n2[s, h, 0, 0] = jnp.sum(n1[s, h], axis=0)
        for slot in reversed(range(nz)):
            dz = offs[slot]
            for dv in range(2):
                if dv or dz:
                    send(s, h, "n2", dv * nz + dz, n2.at[s, h, 0, 0], n2.at[s, h, dv, dz], (dv, 0, 0, dz))

    columns = [slice(h * LANES, (h + 1) * LANES) for h in range(blocks)]

    def gradient(s, h):
        arrive(s, h, "swap", 0)
        for dv in range(2):
            for dz in range(nz):
                if dv or dz:
                    arrive(s, h, "n2", dv * nz + dz)
        own_scale = lax.rsqrt(jnp.sum(n2[s, h, 0], axis=0) / total_rows + EPSILON)
        other_scale = lax.rsqrt(jnp.sum(n2[s, h, 1], axis=0) / total_rows + EPSILON)
        own = (pf[s, h] * own_scale).astype(jnp.bfloat16)
        other = (pp[s, h] * other_scale).astype(jnp.bfloat16)
        rr[h] = (own.astype(jnp.float32) - other.astype(jnp.float32)).astype(jnp.bfloat16)
        for g in (1, 0):
            for e in by_m:
                for p in range(2):
                    part = jnp.dot(xt[p, g, :, e].reshape(n * span, rows), rr[h], preferred_element_type=jnp.float32)
                    gs[s, h, p, g, e] = part.astype(jnp.bfloat16).reshape(n, near, PIECE, LANES)
                    for d in others:
                        send(s, h, "r1", ((p * 2 + g) * n + e) * n + d, gs.at[s, h, p, g, e, d],
                             r1.at[s, h, p, g, e, d - 1], along_l(p, d))
        own_w[h] = own_w[h] * own_scale
        if s == ITERS - 1:
            proj_ref[:, columns[h]] = own

    def wide(value):
        return value.astype(jnp.float32)

    def first_sum(s, h, p, g, e):
        for d in others:
            arrive(s, h, "r1", ((p * 2 + g) * n + e) * n + d)
        total = wide(gs[s, h, p, g, e, 0])
        for d in range(n - 1):
            total += wide(r1[s, h, p, g, e, d])
        return total

    def reduce_2(g, s, h):
        for e in others:
            for p in range(2):
                t2[s, h, p, g, e - 1] = first_sum(s, h, p, g, e).astype(jnp.bfloat16)
                send(s, h, "r2", (p * 2 + g) * n + e, t2.at[s, h, p, g, e - 1], r2.at[s, h, p, g, e - 1], along_m(p, e))

    kept = {}

    def reduce_3(g, s, h):
        for p in range(2):
            total = first_sum(s, h, p, g, 0)
            for e in others:
                arrive(s, h, "r2", (p * 2 + g) * n + e)
                total += wide(r2[s, h, p, g, e - 1])
            t3[s, h, g, :, p] = total.astype(jnp.bfloat16)
            if g == 0:
                kept[h, p] = total[0]
        for slot in reversed(range(g * near, (g + 1) * near)):
            if slot:
                send(s, h, "r3", slot, t3.at[s, h, g, slot % near], r3.at[s, h, slot], (0, 0, 0, offs[slot]))

    def update(s, h):
        for slot in reversed(range(1, nz)):
            arrive(s, h, "r3", slot)
        for p in range(2):
            grad = kept.pop((h, p))
            for slot in range(1, nz):
                grad += wide(r3[s, h, slot, p])
            at = slice(p * PIECE, (p + 1) * PIECE)
            new = root * (own_w[h, at] - STEP_RATE * (grad / total_rows))
            if s == ITERS - 1:
                wout_ref[at, columns[h]] = new
            else:
                own_w[h, at] = new
                wg[s + 1, h, p, 0, 0, 0, 0] = new.astype(jnp.bfloat16)
        if s < ITERS - 1:
            gather_z(s + 1, h)

    def choose():
        i = lax.broadcasted_iota(jnp.int32, (strip, strip), 0)
        j = lax.broadcasted_iota(jnp.int32, (strip, strip), 1)
        slot = j // (strip // 2) * near + lax.rem(j // PIECE, near)
        half = lax.rem(j // span, 2)
        wanted = jnp.zeros_like(slot)
        for k in range(nz):
            wanted = jnp.where(slot == k, offs[k], wanted)
        wanted = lax.rem(wanted + z, nz) * 2 * PIECE + lax.rem(j, PIECE)
        for p in range(2):
            for b in range(2):
                hit = jnp.logical_and(i == wanted + p * PIECE, half == b)
                perm[p, b] = jnp.where(hit, 1.0, 0.0).astype(jnp.bfloat16)

    def turn():
        pairs = n // 2

        def one(i, carry):
            l, mp = i // pairs, lax.rem(i, pairs)
            for p in range(2):
                out = None
                for b in range(2):
                    m = mp * 2 + b
                    dx, dy = (l, m) if p == 0 else (m, l)
                    place = (lax.rem(x + dx, n) * n + lax.rem(y + dy, n)) * strip
                    lanes = pl.ds(pl.multiple_of(place, strip), strip)
                    part = jnp.dot(xs[:, lanes], perm[p, b], preferred_element_type=jnp.float32)
                    out = part if out is None else out + part
                out = out.astype(jnp.bfloat16)
                for g in range(2):
                    some = out[:, g * 2 * span:(g + 1) * 2 * span]
                    to = pl.multiple_of(i * 2 * span, 2 * span)
                    xp[p, g, :, pl.ds(to, 2 * span)] = some
                    xt[p, g, l, pl.ds(mp * 2, 2)] = some.T.reshape(2, span, rows)
            return carry

        lax.fori_loop(0, n * pairs, one, 0)

    load_w.wait()
    for h in range(blocks):
        own_w[h] = w_in[:, columns[h]]
        for p in range(2):
            wg[0, h, p, 0, 0, 0, 0] = own_w[h, p * PIECE:(p + 1) * PIECE].astype(jnp.bfloat16)
    pl.semaphore_wait(barrier, len(partners))
    for h in range(blocks):
        gather_z(0, h)
    choose()

    stages = (
        functools.partial(gather_m, 0),
        functools.partial(gather_m, 1),
        functools.partial(gather_l, 0),
        functools.partial(gather_l, 1),
        functools.partial(project, 0),
        functools.partial(project, 1),
        norm_2,
        gradient,
        functools.partial(reduce_2, 1),
        functools.partial(reduce_2, 0),
        functools.partial(reduce_3, 1),
        functools.partial(reduce_3, 0),
        update,
    )
    for s in range(ITERS):
        for i, stage in enumerate(stages):
            if s == 0 and i == 4:
                load_x.wait()
                turn()
            for h in range(blocks):
                drain(200)
                stage(s, h)
    drain(0)


def on_device(dims, views, weights):
    n, nz = dims
    _, rows, feats = views.shape
    _, own_rows, width = weights.shape
    blocks = width // LANES
    _, count = layout(n, nz)
    near = nz // 2
    strip = nz * 2 * PIECE
    half, full, dma = jnp.bfloat16, jnp.float32, pltpu.SemaphoreType.DMA
    lead = (ITERS, blocks)
    tile = (near, PIECE, LANES)
    scratch = [
        pltpu.VMEM((rows, feats), half),
        pltpu.VMEM((own_rows, width), full),
        pltpu.VMEM((2, 2, strip, strip), half),
        pltpu.VMEM((2, 2, rows, feats // 4), half),
        pltpu.VMEM((2, 2, n, n, near * PIECE, rows), half),
        pltpu.VMEM(lead + (2, 2, n, n) + tile, half),
        pltpu.VMEM(lead + (rows, LANES), full),
        pltpu.VMEM(lead + (rows, LANES), full),
        pltpu.VMEM((blocks, rows, LANES), half),
        pltpu.VMEM(lead + (n * n, 1, LANES), full),
        pltpu.VMEM(lead + (2, nz, 1, LANES), full),
        pltpu.VMEM(lead + (2, 2, n, n) + tile, half),
        pltpu.VMEM(lead + (2, 2, n, n - 1) + tile, half),
        pltpu.VMEM(lead + (2, 2, n - 1) + tile, half),
        pltpu.VMEM(lead + (2, 2, n - 1) + tile, half),
        pltpu.VMEM(lead + (2, near, 2, PIECE, LANES), half),
        pltpu.VMEM(lead + (nz, 2, PIECE, LANES), half),
        pltpu.VMEM((blocks, own_rows, LANES), full),
        dma(lead + (count,)),
        dma(lead + (count,)),
        dma((2,)),
    ]
    total_rows = rows * n * n * nz
    vmem = pl.BlockSpec(memory_space=pltpu.VMEM)
    hbm = pl.BlockSpec(memory_space=pl.ANY)
    flops = 4 * ITERS * rows * feats * width
    new, shown = pl.pallas_call(
        functools.partial(kernel, dims, total_rows, math.sqrt(feats)),
        out_shape=(
            jax.ShapeDtypeStruct((own_rows, width), full),
            jax.ShapeDtypeStruct((rows, width), half),
        ),
        in_specs=[hbm, hbm],
        out_specs=(vmem, vmem),
        scratch_shapes=scratch,
        compiler_params=pltpu.CompilerParams(
            collective_id=0, has_side_effects=True, vmem_limit_bytes=56 << 20
        ),
        cost_estimate=pl.CostEstimate(flops=flops, bytes_accessed=2 * rows * feats, transcendentals=0),
        name="cca_steps",
    )(views[0], weights[0])
    return new[None], shown[None]


def solution(mesh):
    dims = (math.isqrt(mesh.shape["row"]), mesh.shape["feat"])
    spec = P("view", ("row", "feat"), None)
    return jax.shard_map(
        functools.partial(on_device, dims),
        mesh=mesh,
        in_specs=(spec, spec),
        out_specs=(spec, spec),
        check_vma=False,
    )
```

```python
import functools
import math

import jax
import jax.numpy as jnp
from jax import lax
from jax.experimental import pallas as pl
from jax.experimental.pallas import tpu as pltpu
from jax.sharding import PartitionSpec as P

ITERS = 2
EPSILON = 1e-06
STEP_RATE = 0.5
TURN_AT = 4
WIDE = 256
HALF = 128
PIECE = 16
MESH = pl.DeviceIdType.MESH
ODD_0, EVEN_0, EVEN_1 = range(3)


def arrivals(n):
    sizes = {
        "gz": 2,
        "gm": 2 * n,
        "gl": 2 * n,
        "zf": n,
        "n1": 1,
        "n2": ITERS,
        "swap": ITERS,
        "rz": n,
        "r1": 3 * n,
        "r2": 3,
        "r3": 2,
    }
    start, places = 0, {}
    for name, count in sizes.items():
        places[name] = start
        start += count
    return places, start


DEPARTURES = ("gz0", "gz1", "gm0", "gm1", "gl0", "gl1", "zf", "n1", "n2", "swap", "rz", "r1", "r2", "r30", "r31")


def slots(nz):
    reach = nz // 4
    even = [2 * i for i in reversed(range(reach))] + [-2 * i for i in range(1, reach)] + [2 * reach]
    odd = [2 * i + 1 for i in reversed(range(reach))] + [-2 * i - 1 for i in range(reach)]
    return [d % nz for d in even + odd], reach


def kernel(dims, total_rows, root, x_hbm, w_hbm, wout_ref, proj_ref, *scratch):
    n, nz = dims
    (xs, own_w, perm, xp, xt, wg, pf, pp, rr, n1, n2, gs, go, rz, r1, t2, r2, t3, t3o, r3, r3o,
     send_sem, recv_sem, load_sem) = scratch
    rows, feats = xs.shape
    near = nz // 2
    offs, reach = slots(nz)
    mine = reach - 1
    first, second = pl.ds(0, HALF), pl.ds(HALF, HALF)
    up, down = pl.ds(0, reach), pl.ds(mine, reach)
    odd_up, odd_down = pl.ds(0, reach), pl.ds(reach, reach)
    places, _ = arrivals(n)
    strip = nz * 2 * PIECE
    span = near * PIECE
    others = sorted(range(1, n), key=lambda d: (min(d, n - d), d))
    by_m = others + [0]

    v = lax.axis_index("view")
    r = lax.axis_index("row")
    z = lax.axis_index("feat")
    x, y = r // n, lax.rem(r, n)

    def ahead(i, d, size):
        return lax.rem(i + d, size) if d else i

    def device(dv, dx, dy, dz):
        return (ahead(v, dv, 2), ahead(x, dx, n) * n + ahead(y, dy, n), ahead(z, dz, nz))

    def along_l(p, d):
        return (0, d, 0, 0) if p == 0 else (0, 0, d, 0)

    def along_m(p, d):
        return (0, 0, d, 0) if p == 0 else (0, d, 0, 0)

    partners = [(0, dx, dy, 0) for dx in range(n) for dy in range(n) if dx or dy]
    partners += [(dv, 0, 0, dz) for dv in range(2) for dz in range(nz) if dv or dz]

    barrier = pltpu.get_barrier_semaphore()
    for to in partners:
        pl.semaphore_signal(barrier, inc=1, device_id=device(*to), device_id_type=MESH)
    load_w = pltpu.make_async_copy(w_hbm, own_w, load_sem.at[1])
    load_w.start()
    load_x = pltpu.make_async_copy(x_hbm, xs, load_sem.at[0])
    load_x.start()

    def sent(s, name):
        g = int(name[2:]) if name[:2] in ("gz", "gm", "gl", "r3") else 0
        rest = pl.ds(1, n - 1)
        wide_or_half = wg.at[s, :, g] if g == 0 else wg.at[s, :, g, :, :, :, :, first]
        return {
            "gz": wg.at[s, :, 0, 0, 0, pl.ds(0, near - 1)] if g == 0 else wg.at[s, :, 1, 0, 0, :, :, first],
            "gm": wide_or_half.at[:, 0, rest],
            "gl": wide_or_half.at[:, rest],
            "zf": wg.at[s, :, 1, :, :, :, :, second],
            "n1": n1.at[s, pl.ds(1, n * n - 1)],
            "n2": n2.at[s, pl.ds(1, 2 * nz - 1)],
            "sw": pp.at[s],
            "rz": rz.at[s],
            "r1": r1.at[s],
            "r2": r2.at[s],
            "r3": r3.at[s, pl.ds(0, near - 1)] if g == 0 else r3o.at[s],
        }[name[:2]]

    def copy_of(src, dst, out, name, index, to):
        return pltpu.make_async_remote_copy(
            src_ref=src,
            dst_ref=dst,
            send_sem=send_sem.at[DEPARTURES.index(out)],
            recv_sem=recv_sem.at[places[name] + index],
            device_id=device(*to),
            device_id_type=MESH,
        )

    busy = {}

    def leave(out):
        if out in busy:
            whole = sent(busy.pop(out), out)
            copy_of(whole, whole, out, "gz", 0, (1, 0, 0, 0)).wait_send()

    def send(s, out, index, src, dst, to):
        if busy.get(out, s) != s:
            leave(out)
        busy[out] = s
        name = out if out in places else out[:2]
        copy_of(src, dst, out, name, index, to).start()

    def arrive(name, index, whole):
        copy_of(whole, whole, "gz0", name, index, (1, 0, 0, 0)).wait_recv()

    def part_of(s, p, g, d, e):
        return wg.at[s, p, g, d, e] if g == 0 else wg.at[s, p, g, d, e, :, :, first]

    def gather_z(s):
        for slot in sorted(range(nz), key=lambda k: (k // near, -min(offs[k], nz - offs[k]))):
            if slot == mine:
                continue
            g = slot // near
            for p in range(2):
                src = wg.at[s, p, 0, 0, 0, mine]
                dst = wg.at[s, p, g, 0, 0, slot % near]
                if g:
                    src, dst = src.at[:, first], dst.at[:, first]
                send(s, f"gz{g}", g, src, dst, (0, 0, 0, nz - offs[slot]))

    def forward(s, d):
        for p in range(2):
            even, odd = wg.at[s, p, 0, d], wg.at[s, p, 1, d]
            send(s, "zf", d, even.at[:, up, :, second], odd.at[:, odd_up, :, second], (0, 0, 0, nz - 1))
            send(s, "zf", d, even.at[:, down, :, second], odd.at[:, odd_down, :, second], (0, 0, 0, 1))

    def gather_m(g, s):
        arrive("gz", g, sent(s, f"gz{g}"))
        for p in range(2):
            src = part_of(s, p, g, 0, 0)
            for e in others:
                send(s, f"gm{g}", g * n + e, src, part_of(s, p, g, 0, e), along_m(p, n - e))
        for p in range(2):
            src = part_of(s, p, g, 0, 0)
            for d in others:
                send(s, f"gl{g}", g * n + d, src, part_of(s, p, g, d, 0), along_l(p, n - d))

    def both(s, g):
        return wg.at[s, :, 0] if g == 0 else wg.at[s, :, 1, :, :, :, :, first]

    def gather_l(g, s):
        for e in others:
            arrive("gm", g * n + e, both(s, g).at[:, 0, e])
            for p in range(2):
                src = part_of(s, p, g, 0, e)
                for d in others:
                    send(s, f"gl{g}", g * n + d, src, part_of(s, p, g, d, e), along_l(p, n - d))
        if g == 0:
            forward(s, 0)

    def gather_far(s):
        for d in others:
            arrive("gl", d, both(s, 0).at[:, d])
            forward(s, d)

    def project(g, s):
        for d in [0] + others:
            if g:
                if d:
                    arrive("gl", n + d, both(s, 1).at[:, d])
                arrive("zf", d, wg.at[s, :, 1, d, :, :, :, second])
            for p in range(2):
                width = n * span
                part = jnp.dot(
                    xp[p, g, :, d * width:(d + 1) * width],
                    wg[s, p, g, d].reshape(width, WIDE),
                    preferred_element_type=jnp.float32,
                )
                if g or d or p:
                    part += pf[s]
                pf[s] = part

    def norm_1(s):
        part = pf[s]
        n1[s, 0] = jnp.sum(part * part, axis=0, keepdims=True)
        for dx in range(n):
            for dy in range(n):
                if dx or dy:
                    send(s, "n1", 0, n1.at[s, 0], n1.at[s, dx * n + dy], (0, dx, dy, 0))
        send(s, "swap", s, pf.at[s], pp.at[s], (1, 0, 0, 0))

    def norm_2(s):
        arrive("n1", 0, sent(s, "n1"))
        n2[s, 0] = jnp.sum(n1[s], axis=0)
        for dz in sorted(range(nz), key=lambda d: -min(d, nz - d)):
            for dv in range(2):
                if dv or dz:
                    send(s, "n2", s, n2.at[s, 0], n2.at[s, dv * nz + dz], (dv, 0, 0, dz))

    def wide(value):
        return value.astype(jnp.float32)

    def spread(s, k, p, e):
        for d in others:
            send(s, "r1", k * n + e, gs.at[s, k, p, e, d], r1.at[s, k, e, p, d - 1], along_l(p, d))

    def gradient(s):
        arrive("swap", s, pp.at[s])
        arrive("n2", s, sent(s, "n2"))
        own_scale = lax.rsqrt(jnp.sum(n2[s, :nz], axis=0) / total_rows + EPSILON)
        other_scale = lax.rsqrt(jnp.sum(n2[s, nz:], axis=0) / total_rows + EPSILON)
        own = (pf[s] * own_scale).astype(jnp.bfloat16)
        other = (pp[s] * other_scale).astype(jnp.bfloat16)
        rr[...] = (wide(own) - wide(other)).astype(jnp.bfloat16)
        for g in (1, 0):
            for e in by_m:
                for p in range(2):
                    part = jnp.dot(xt[p, g, :, e].reshape(n * span, rows), rr[...], preferred_element_type=jnp.float32)
                    part = part.astype(jnp.bfloat16).reshape(n, near, PIECE, WIDE)
                    gs[s, EVEN_0 if g == 0 else ODD_0, p, e] = part[..., :HALF]
                    if g == 0:
                        gs[s, EVEN_1, p, e] = part[..., HALF:]
                        spread(s, EVEN_0, p, e)
                    else:
                        go[s, p, e] = part[..., HALF:]
                        send(s, "rz", e, go.at[s, p, e, :, odd_up], rz.at[s, e, p, 0], (0, 0, 0, 1))
                        send(s, "rz", e, go.at[s, p, e, :, odd_down], rz.at[s, e, p, 1], (0, 0, 0, nz - 1))
                        spread(s, ODD_0, p, e)
        own_w[...] = own_w[...] * own_scale
        if s == ITERS - 1:
            proj_ref[...] = own

    def reduce_z(s):
        for e in by_m:
            arrive("rz", e, rz.at[s, e])
            for p in range(2):
                for k in range(near):
                    total = wide(gs[s, EVEN_1, p, e, :, k])
                    if k < reach:
                        total += wide(rz[s, e, p, 0, :, k])
                    if mine <= k < mine + reach:
                        total += wide(rz[s, e, p, 1, :, k - mine])
                    if k < mine + reach:
                        gs[s, EVEN_1, p, e, :, k] = total.astype(jnp.bfloat16)
                spread(s, EVEN_1, p, e)

    def first_sum(s, k, p, e):
        if p == 0:
            arrive("r1", k * n + e, r1.at[s, k, e])
        total = wide(gs[s, k, p, e, 0])
        for d in range(n - 1):
            total += wide(r1[s, k, e, p, d])
        return total

    def reduce_2(k, s):
        for e in others:
            for p in range(2):
                t2[s, k, p, e - 1] = first_sum(s, k, p, e).astype(jnp.bfloat16)
                send(s, "r2", k, t2.at[s, k, p, e - 1], r2.at[s, k, p, e - 1], along_m(p, e))

    kept = {}

    def second_sum(s, k, p):
        total = first_sum(s, k, p, 0)
        if p == 0:
            arrive("r2", k, r2.at[s, k])
        for e in others:
            total += wide(r2[s, k, p, e - 1])
        if k != ODD_0:
            kept[k, p] = total[mine]
        return total.astype(jnp.bfloat16)

    def reduce_3(g, s):
        for p in range(2):
            if g:
                t3o[s, :, p] = second_sum(s, ODD_0, p)
            else:
                t3[s, :, p, :, :HALF] = second_sum(s, EVEN_0, p)
                t3[s, :, p, :, HALF:] = second_sum(s, EVEN_1, p)
        for slot in sorted(range(g * near, (g + 1) * near), key=lambda k: -min(offs[k], nz - offs[k])):
            k = slot % near
            if g:
                send(s, "r31", 1, t3o.at[s, k], r3o.at[s, k], (0, 0, 0, offs[slot]))
            elif slot != mine:
                send(s, "r30", 0, t3.at[s, k], r3.at[s, k - (k > mine)], (0, 0, 0, offs[slot]))

    def update(s):
        arrive("r3", 1, r3o.at[s])
        arrive("r3", 0, sent(s, "r30"))
        for p in range(2):
            at = slice(p * PIECE, (p + 1) * PIECE)
            for c, k in enumerate((EVEN_0, EVEN_1)):
                columns = slice(c * HALF, (c + 1) * HALF)
                grad = kept.pop((k, p))
                for slot in range(near):
                    if slot != mine:
                        grad += wide(r3[s, slot - (slot > mine), p, :, columns])
                    if c == 0:
                        grad += wide(r3o[s, slot, p])
                new = root * (own_w[at, columns] - STEP_RATE * (grad / total_rows))
                if s == ITERS - 1:
                    wout_ref[at, columns] = new
                else:
                    own_w[at, columns] = new
                    wg[s + 1, p, 0, 0, 0, mine, :, columns] = new.astype(jnp.bfloat16)
        if s < ITERS - 1:
            gather_z(s + 1)

    def choose():
        i = lax.broadcasted_iota(jnp.int32, (strip, strip), 0)
        j = lax.broadcasted_iota(jnp.int32, (strip, strip), 1)
        slot = j // (strip // 2) * near + lax.rem(j // PIECE, near)
        half = lax.rem(j // span, 2)
        wanted = jnp.zeros_like(slot)
        for k in range(nz):
            wanted = jnp.where(slot == k, offs[k], wanted)
        wanted = lax.rem(wanted + z, nz) * 2 * PIECE + lax.rem(j, PIECE)
        for p in range(2):
            for b in range(2):
                hit = jnp.logical_and(i == wanted + p * PIECE, half == b)
                perm[p, b] = jnp.where(hit, 1.0, 0.0).astype(jnp.bfloat16)

    def turn():
        pairs = n // 2

        def one(i, carry):
            l, mp = i // pairs, lax.rem(i, pairs)
            for p in range(2):
                out = None
                for b in range(2):
                    m = mp * 2 + b
                    dx, dy = (l, m) if p == 0 else (m, l)
                    place = (lax.rem(x + dx, n) * n + lax.rem(y + dy, n)) * strip
                    lanes = pl.ds(pl.multiple_of(place, strip), strip)
                    part = jnp.dot(xs[:, lanes], perm[p, b], preferred_element_type=jnp.float32)
                    out = part if out is None else out + part
                out = out.astype(jnp.bfloat16)
                for g in range(2):
                    some = out[:, g * 2 * span:(g + 1) * 2 * span]
                    to = pl.multiple_of(i * 2 * span, 2 * span)
                    xp[p, g, :, pl.ds(to, 2 * span)] = some
                    xt[p, g, l, pl.ds(mp * 2, 2)] = some.T.reshape(2, span, rows)
            return carry

        lax.fori_loop(0, n * pairs, one, 0)

    load_w.wait()
    for p in range(2):
        wg[0, p, 0, 0, 0, mine] = own_w[p * PIECE:(p + 1) * PIECE, :].astype(jnp.bfloat16)
    pl.semaphore_wait(barrier, len(partners))
    gather_z(0)
    choose()

    stages = (
        functools.partial(gather_m, 0),
        functools.partial(gather_m, 1),
        functools.partial(gather_l, 0),
        functools.partial(gather_l, 1),
        gather_far,
        functools.partial(project, 0),
        functools.partial(project, 1),
        norm_1,
        norm_2,
        gradient,
        reduce_z,
        functools.partial(reduce_2, ODD_0),
        functools.partial(reduce_2, EVEN_0),
        functools.partial(reduce_2, EVEN_1),
        functools.partial(reduce_3, 1),
        functools.partial(reduce_3, 0),
        update,
    )
    for s in range(ITERS):
        for i, stage in enumerate(stages):
            if s == 0 and i == TURN_AT:
                load_x.wait()
                turn()
            stage(s)
    for out in DEPARTURES:
        leave(out)


def on_device(dims, views, weights):
    n, nz = dims
    _, rows, feats = views.shape
    _, own_rows, width = weights.shape
    _, count = arrivals(n)
    near, reach = nz // 2, nz // 4
    strip = nz * 2 * PIECE
    half, full, dma = jnp.bfloat16, jnp.float32, pltpu.SemaphoreType.DMA
    lead = (ITERS,)
    tile = (near, PIECE, HALF)
    scratch = [
        pltpu.VMEM((rows, feats), half),
        pltpu.VMEM((own_rows, width), full),
        pltpu.VMEM((2, 2, strip, strip), half),
        pltpu.VMEM((2, 2, rows, feats // 4), half),
        pltpu.VMEM((2, 2, n, n, near * PIECE, rows), half),
        pltpu.VMEM(lead + (2, 2, n, n, near, PIECE, width), half),
        pltpu.VMEM(lead + (rows, width), full),
        pltpu.VMEM(lead + (rows, width), full),
        pltpu.VMEM((rows, width), half),
        pltpu.VMEM(lead + (n * n, 1, width), full),
        pltpu.VMEM(lead + (2 * nz, 1, width), full),
        pltpu.VMEM(lead + (3, 2, n, n) + tile, half),
        pltpu.VMEM(lead + (2, n, n) + tile, half),
        pltpu.VMEM(lead + (n, 2, 2, n, reach, PIECE, HALF), half),
        pltpu.VMEM(lead + (3, n, 2, n - 1) + tile, half),
        pltpu.VMEM(lead + (3, 2, n - 1) + tile, half),
        pltpu.VMEM(lead + (3, 2, n - 1) + tile, half),
        pltpu.VMEM(lead + (near, 2, PIECE, width), half),
        pltpu.VMEM(lead + (near, 2, PIECE, HALF), half),
        pltpu.VMEM(lead + (near, 2, PIECE, width), half),
        pltpu.VMEM(lead + (near, 2, PIECE, HALF), half),
        dma((len(DEPARTURES),)),
        dma((count,)),
        dma((2,)),
    ]
    total_rows = rows * n * n * nz
    vmem = pl.BlockSpec(memory_space=pltpu.VMEM)
    hbm = pl.BlockSpec(memory_space=pl.ANY)
    flops = 4 * ITERS * rows * feats * width
    new, shown = pl.pallas_call(
        functools.partial(kernel, dims, total_rows, math.sqrt(feats)),
        out_shape=(
            jax.ShapeDtypeStruct((own_rows, width), full),
            jax.ShapeDtypeStruct((rows, width), half),
        ),
        in_specs=[hbm, hbm],
        out_specs=(vmem, vmem),
        scratch_shapes=scratch,
        compiler_params=pltpu.CompilerParams(
            collective_id=0, has_side_effects=True, vmem_limit_bytes=56 << 20
        ),
        cost_estimate=pl.CostEstimate(flops=flops, bytes_accessed=2 * rows * feats, transcendentals=0),
        name="cca_steps",
    )(views[0], weights[0])
    return new[None], shown[None]


def solution(mesh):
    dims = (math.isqrt(mesh.shape["row"]), mesh.shape["feat"])
    spec = P("view", ("row", "feat"), None)
    return jax.shard_map(
        functools.partial(on_device, dims),
        mesh=mesh,
        in_specs=(spec, spec),
        out_specs=(spec, spec),
        check_vma=False,
    )
```

```python
import functools
import math

import jax
import jax.numpy as jnp
from jax import lax
from jax.experimental import pallas as pl
from jax.experimental.pallas import tpu as pltpu
from jax.sharding import PartitionSpec as P

ITERS = 2
EPSILON = 1e-06
STEP_RATE = 0.5
WIDE = 256
HALF = 128
PIECE = 16
MESH = pl.DeviceIdType.MESH
ODD_0, EVEN_0, EVEN_1, AHEAD = range(4)


def arrivals(n):
    sizes = {
        "gz": 3,
        "gm": 4 * n,
        "gl": 2 * n,
        "zf": n,
        "n1": 1,
        "n2": ITERS,
        "swap": ITERS,
        "rz": n,
        "r1": 4 * n,
        "r2": 4,
        "r3": 2,
    }
    start, places = 0, {}
    for name, count in sizes.items():
        places[name] = start
        start += count
    return places, start


DEPARTURES = ("gz0", "gz1", "gm0", "gm1", "gl0", "gl1", "zf", "n1", "n2", "swap", "rz", "r1", "r2", "r30", "r31")


def slots(nz):
    reach = nz // 4
    even = [2 * i for i in reversed(range(reach))] + [-2 * i for i in range(1, reach)] + [2 * reach]
    odd = [2 * i + 1 for i in reversed(range(reach))] + [-2 * i - 1 for i in range(reach)]
    return [d % nz for d in even + odd], reach


def kernel(dims, total_rows, root, x_hbm, w_hbm, wout_ref, proj_ref, *scratch):
    n, nz = dims
    (xs, own_w, perm, xp, xt, wg, pf, pp, rr, n1, n2, gs, go, rz, r1, t2, r2, t3, t3o, r3, r3o,
     send_sem, recv_sem, load_sem) = scratch
    rows, feats = xs.shape
    near = nz // 2
    offs, reach = slots(nz)
    mine = reach - 1
    groups = [[mine], [k for k in range(near - 1) if k != mine], [near - 1]]
    odd_group = len(groups)
    first, second = pl.ds(0, HALF), pl.ds(HALF, HALF)
    up, down = pl.ds(0, reach), pl.ds(mine, reach)
    odd_up, odd_down = pl.ds(0, reach), pl.ds(reach, reach)
    places, _ = arrivals(n)
    strip = nz * 2 * PIECE
    span = near * PIECE
    others = sorted(range(1, n), key=lambda d: (min(d, n - d), d))
    far_first = sorted(others, key=lambda d: -min(d, n - d))
    by_m = far_first + [0]
    extent = {ODD_0: (ODD_0, 0, near), EVEN_0: (EVEN_0, 0, near), EVEN_1: (EVEN_1, 0, near - 1), AHEAD: (EVEN_1, near - 1, near)}

    v = lax.axis_index("view")
    r = lax.axis_index("row")
    z = lax.axis_index("feat")
    x, y = r // n, lax.rem(r, n)

    def ahead(i, d, size):
        return lax.rem(i + d, size) if d else i

    def device(dv, dx, dy, dz):
        return (ahead(v, dv, 2), ahead(x, dx, n) * n + ahead(y, dy, n), ahead(z, dz, nz))

    def along_l(p, d):
        return (0, d, 0, 0) if p == 0 else (0, 0, d, 0)

    def along_m(p, d):
        return (0, 0, d, 0) if p == 0 else (0, d, 0, 0)

    partners = [(0, dx, dy, 0) for dx in range(n) for dy in range(n) if dx or dy]
    partners += [(dv, 0, 0, dz) for dv in range(2) for dz in range(nz) if dv or dz]

    barrier = pltpu.get_barrier_semaphore()
    for to in partners:
        pl.semaphore_signal(barrier, inc=1, device_id=device(*to), device_id_type=MESH)
    load_w = pltpu.make_async_copy(w_hbm, own_w, load_sem.at[1])
    load_w.start()
    load_x = pltpu.make_async_copy(x_hbm, xs, load_sem.at[0])
    load_x.start()

    def sent(s, name):
        g = int(name[2:]) if name[:2] in ("gz", "gm", "gl", "r3") else 0
        rest = pl.ds(1, n - 1)
        wide_or_half = wg.at[s, :, g] if g == 0 else wg.at[s, :, g, :, :, :, :, first]
        return {
            "gz": wg.at[s, :, 0, 0, 0, pl.ds(0, near - 1)] if g == 0 else wg.at[s, :, 1, 0, 0, :, :, first],
            "gm": wide_or_half.at[:, 0, rest],
            "gl": wide_or_half.at[:, rest],
            "zf": wg.at[s, :, 1, :, :, :, :, second],
            "n1": n1.at[s, pl.ds(1, n * n - 1)],
            "n2": n2.at[s, pl.ds(1, 2 * nz - 1)],
            "sw": pp.at[s],
            "rz": rz.at[s],
            "r1": r1.at[s],
            "r2": r2.at[s],
            "r3": r3.at[s, pl.ds(0, near - 1)] if g == 0 else r3o.at[s],
        }[name[:2]]

    def copy_of(src, dst, out, name, index, to):
        return pltpu.make_async_remote_copy(
            src_ref=src,
            dst_ref=dst,
            send_sem=send_sem.at[DEPARTURES.index(out)],
            recv_sem=recv_sem.at[places[name] + index],
            device_id=device(*to),
            device_id_type=MESH,
        )

    busy = {}

    def leave(out):
        if out in busy:
            whole = sent(busy.pop(out), out)
            copy_of(whole, whole, out, "gz", 0, (1, 0, 0, 0)).wait_send()

    def send(s, out, index, src, dst, to):
        if busy.get(out, s) != s:
            leave(out)
        busy[out] = s
        name = out if out in places else out[:2]
        copy_of(src, dst, out, name, index, to).start()

    def arrive(name, index, whole):
        copy_of(whole, whole, "gz0", name, index, (1, 0, 0, 0)).wait_recv()

    def part_of(s, p, g, d, e):
        return wg.at[s, p, g, d, e] if g == 0 else wg.at[s, p, g, d, e, :, :, first]

    def rows_of(s, p, d, e, group):
        if group == odd_group:
            return [part_of(s, p, 1, d, e)]
        return [wg.at[s, p, 0, d, e, k] for k in groups[group]]

    def gather_z(s):
        for group in (1, 2, odd_group):
            g = group // odd_group
            for k in range(near) if g else groups[group]:
                for p in range(2):
                    src = wg.at[s, p, 0, 0, 0, mine]
                    dst = wg.at[s, p, g, 0, 0, k]
                    if g:
                        src, dst = src.at[:, first], dst.at[:, first]
                    send(s, f"gz{g}", group - 1, src, dst, (0, 0, 0, nz - offs[g * near + k]))

    def forward(s, d):
        for p in range(2):
            even, odd = wg.at[s, p, 0, d], wg.at[s, p, 1, d]
            send(s, "zf", d, even.at[:, up, :, second], odd.at[:, odd_up, :, second], (0, 0, 0, nz - 1))
            send(s, "zf", d, even.at[:, down, :, second], odd.at[:, odd_down, :, second], (0, 0, 0, 1))

    def both(s, g):
        return wg.at[s, :, 0] if g == 0 else wg.at[s, :, 1, :, :, :, :, first]

    def gather_m(group, s):
        g = group // odd_group
        if g:
            arrive("gz", group - 1, sent(s, "gz1"))
        elif group:
            arrive("gz", group - 1, wg.at[s, :, 0, 0, 0, pl.ds(0, len(groups[group]))])
        for p in range(2):
            for e in far_first:
                for src, dst in zip(rows_of(s, p, 0, 0, group), rows_of(s, p, 0, e, group)):
                    send(s, f"gm{g}", group * n + e, src, dst, along_m(p, n - e))
        for p in range(2):
            for d in far_first:
                for src, dst in zip(rows_of(s, p, 0, 0, group), rows_of(s, p, d, 0, group)):
                    send(s, f"gl{g}", g * n + d, src, dst, along_l(p, n - d))

    def gather_l(group, s):
        g = group // odd_group
        for e in others:
            here = both(s, g).at[:, 0, e]
            arrive("gm", group * n + e, here if g else here.at[:, pl.ds(0, len(groups[group]))])
            for p in range(2):
                for d in far_first:
                    for src, dst in zip(rows_of(s, p, 0, e, group), rows_of(s, p, d, e, group)):
                        send(s, f"gl{g}", g * n + d, src, dst, along_l(p, n - d))
        if group == odd_group - 1:
            forward(s, 0)

    def gather_far(s):
        for d in others:
            arrive("gl", d, both(s, 0).at[:, d])
            forward(s, d)

    def project(g, s):
        for d in [0] + others:
            if g:
                if d:
                    arrive("gl", n + d, both(s, 1).at[:, d])
                arrive("zf", d, wg.at[s, :, 1, d, :, :, :, second])
            for p in range(2):
                width = n * span
                part = jnp.dot(
                    xp[p, g, :, d * width:(d + 1) * width],
                    wg[s, p, g, d].reshape(width, WIDE),
                    preferred_element_type=jnp.float32,
                )
                if g or d or p:
                    part += pf[s]
                pf[s] = part

    def norm_1(s):
        part = pf[s]
        n1[s, 0] = jnp.sum(part * part, axis=0, keepdims=True)
        far = lambda d: -min(d // n, n - d // n) - min(d % n, n - d % n)
        for to in sorted(range(1, n * n), key=far):
            send(s, "n1", 0, n1.at[s, 0], n1.at[s, to], (0, to // n, to % n, 0))
        send(s, "swap", s, pf.at[s], pp.at[s], (1, 0, 0, 0))

    def norm_2(s):
        arrive("n1", 0, sent(s, "n1"))
        n2[s, 0] = jnp.sum(n1[s], axis=0)
        for dz in sorted(range(nz), key=lambda d: -min(d, nz - d)):
            for dv in range(2):
                if dv or dz:
                    send(s, "n2", s, n2.at[s, 0], n2.at[s, dv * nz + dz], (dv, 0, 0, dz))

    def wide(value):
        return value.astype(jnp.float32)

    def within(i):
        k, low, high = extent[i]
        return k, pl.ds(low, high - low)

    def spread(s, i, p, e):
        k, part = within(i)
        for d in far_first:
            send(s, "r1", i * n + e, gs.at[s, k, p, e, d, part], r1.at[s, k, e, p, d - 1, part], along_l(p, d))

    def gradient(s):
        arrive("swap", s, pp.at[s])
        arrive("n2", s, sent(s, "n2"))
        own_scale = lax.rsqrt(jnp.sum(n2[s, :nz], axis=0) / total_rows + EPSILON)
        other_scale = lax.rsqrt(jnp.sum(n2[s, nz:], axis=0) / total_rows + EPSILON)
        own = (pf[s] * own_scale).astype(jnp.bfloat16)
        other = (pp[s] * other_scale).astype(jnp.bfloat16)
        rr[...] = (wide(own) - wide(other)).astype(jnp.bfloat16)
        for g in (1, 0):
            for e in by_m:
                for p in range(2):
                    part = jnp.dot(xt[p, g, :, e].reshape(n * span, rows), rr[...], preferred_element_type=jnp.float32)
                    part = part.astype(jnp.bfloat16).reshape(n, near, PIECE, WIDE)
                    gs[s, EVEN_0 if g == 0 else ODD_0, p, e] = part[..., :HALF]
                    if g == 0:
                        gs[s, EVEN_1, p, e] = part[..., HALF:]
                        spread(s, EVEN_0, p, e)
                        spread(s, AHEAD, p, e)
                    else:
                        go[s, p, e] = part[..., HALF:]
                        send(s, "rz", e, go.at[s, p, e, :, odd_up], rz.at[s, e, p, 0], (0, 0, 0, 1))
                        send(s, "rz", e, go.at[s, p, e, :, odd_down], rz.at[s, e, p, 1], (0, 0, 0, nz - 1))
                        spread(s, ODD_0, p, e)
        own_w[...] = own_w[...] * own_scale
        if s == ITERS - 1:
            proj_ref[...] = own

    def reduce_z(some, s):
        for e in some:
            arrive("rz", e, rz.at[s, e])
            for p in range(2):
                for k in range(near - 1):
                    total = wide(gs[s, EVEN_1, p, e, :, k])
                    if k < reach:
                        total += wide(rz[s, e, p, 0, :, k])
                    if k >= mine:
                        total += wide(rz[s, e, p, 1, :, k - mine])
                    gs[s, EVEN_1, p, e, :, k] = total.astype(jnp.bfloat16)
                spread(s, EVEN_1, p, e)

    def first_sum(s, i, p, e):
        k, part = within(i)
        if p == 0:
            arrive("r1", i * n + e, r1.at[s, k, e, :, :, part])
        total = wide(gs[s, k, p, e, 0, part])
        for d in range(n - 1):
            total += wide(r1[s, k, e, p, d, part])
        return total

    def reduce_2(i, s):
        k, part = within(i)
        for e in far_first:
            for p in range(2):
                t2[s, k, p, e - 1, part] = first_sum(s, i, p, e).astype(jnp.bfloat16)
                send(s, "r2", i, t2.at[s, k, p, e - 1, part], r2.at[s, k, p, e - 1, part], along_m(p, e))

    kept = {}

    def second_sum(s, i, p):
        k, part = within(i)
        total = first_sum(s, i, p, 0)
        if p == 0:
            arrive("r2", i, r2.at[s, k, :, :, part])
        for e in others:
            total += wide(r2[s, k, p, e - 1, part])
        if i in (EVEN_0, EVEN_1):
            kept[i, p] = total[mine]
        return total.astype(jnp.bfloat16)

    def reduce_3_odd(s):
        for p in range(2):
            t3o[s, :, p] = second_sum(s, ODD_0, p)
        for k in sorted(range(near), key=lambda k: -min(offs[near + k], nz - offs[near + k])):
            send(s, "r31", 1, t3o.at[s, k], r3o.at[s, k], (0, 0, 0, offs[near + k]))

    def send_even(s, k):
        send(s, "r30", 0, t3.at[s, k], r3.at[s, k - (k > mine)], (0, 0, 0, offs[k]))

    def reduce_3_ahead(s):
        for p in range(2):
            t3[s, :, p, :, :HALF] = second_sum(s, EVEN_0, p)
            t3[s, near - 1:, p, :, HALF:] = second_sum(s, AHEAD, p)
        send_even(s, near - 1)

    def reduce_3_even(s):
        for p in range(2):
            t3[s, :near - 1, p, :, HALF:] = second_sum(s, EVEN_1, p)
        for k in range(near - 1):
            if k != mine:
                send_even(s, k)

    def update(s):
        arrive("r3", 1, r3o.at[s])
        arrive("r3", 0, sent(s, "r30"))
        for p in range(2):
            at = slice(p * PIECE, (p + 1) * PIECE)
            for c, k in enumerate((EVEN_0, EVEN_1)):
                columns = slice(c * HALF, (c + 1) * HALF)
                grad = kept.pop((k, p))
                for slot in range(near):
                    if slot != mine:
                        grad += wide(r3[s, slot - (slot > mine), p, :, columns])
                    if c == 0:
                        grad += wide(r3o[s, slot, p])
                new = root * (own_w[at, columns] - STEP_RATE * (grad / total_rows))
                if s == ITERS - 1:
                    wout_ref[at, columns] = new
                else:
                    own_w[at, columns] = new
                    wg[s + 1, p, 0, 0, 0, mine, :, columns] = new.astype(jnp.bfloat16)
        if s < ITERS - 1:
            gather_z(s + 1)

    def choose():
        i = lax.broadcasted_iota(jnp.int32, (strip, strip), 0)
        j = lax.broadcasted_iota(jnp.int32, (strip, strip), 1)
        slot = j // (strip // 2) * near + lax.rem(j // PIECE, near)
        half = lax.rem(j // span, 2)
        wanted = jnp.zeros_like(slot)
        for k in range(nz):
            wanted = jnp.where(slot == k, offs[k], wanted)
        wanted = lax.rem(wanted + z, nz) * 2 * PIECE + lax.rem(j, PIECE)
        for p in range(2):
            for b in range(2):
                hit = jnp.logical_and(i == wanted + p * PIECE, half == b)
                perm[p, b] = jnp.where(hit, 1.0, 0.0).astype(jnp.bfloat16)

    def turn(begin, end):
        pairs = n // 2

        def one(i, carry):
            l, mp = i // pairs, lax.rem(i, pairs)
            for p in range(2):
                out = None
                for b in range(2):
                    m = mp * 2 + b
                    dx, dy = (l, m) if p == 0 else (m, l)
                    place = (lax.rem(x + dx, n) * n + lax.rem(y + dy, n)) * strip
                    lanes = pl.ds(pl.multiple_of(place, strip), strip)
                    part = jnp.dot(xs[:, lanes], perm[p, b], preferred_element_type=jnp.float32)
                    out = part if out is None else out + part
                out = out.astype(jnp.bfloat16)
                for g in range(2):
                    some = out[:, g * 2 * span:(g + 1) * 2 * span]
                    to = pl.multiple_of(i * 2 * span, 2 * span)
                    xp[p, g, :, pl.ds(to, 2 * span)] = some
                    xt[p, g, l, pl.ds(mp * 2, 2)] = some.T.reshape(2, span, rows)
            return carry

        lax.fori_loop(begin * n * pairs // 4, end * n * pairs // 4, one, 0)

    load_w.wait()
    for p in range(2):
        wg[0, p, 0, 0, 0, mine] = own_w[p * PIECE:(p + 1) * PIECE, :].astype(jnp.bfloat16)
    pl.semaphore_wait(barrier, len(partners))
    gather_z(0)

    def prepare(begin, end):
        if begin == 0:
            choose()
            load_x.wait()
        turn(begin, end)

    gather = [functools.partial(gather_m, 0), (0, 1), functools.partial(gather_l, 0)]
    gather += [functools.partial(gather_m, k) for k in range(1, odd_group + 1) if k != 1 or groups[1]]
    gather += [(1, 2)]
    gather += [functools.partial(gather_l, k) for k in range(1, odd_group + 1) if k != 1 or groups[1]]
    gather += [(2, 4)]
    stages = gather + [
        gather_far,
        functools.partial(project, 0),
        functools.partial(project, 1),
        norm_1,
        norm_2,
        gradient,
        functools.partial(reduce_z, by_m[:-1]),
        functools.partial(reduce_2, ODD_0),
        functools.partial(reduce_z, by_m[-1:]),
        functools.partial(reduce_2, EVEN_0),
        functools.partial(reduce_2, AHEAD),
        functools.partial(reduce_2, EVEN_1),
        reduce_3_odd,
        reduce_3_ahead,
        reduce_3_even,
        update,
    ]
    for s in range(ITERS):
        for stage in stages:
            if not isinstance(stage, tuple):
                stage(s)
            elif s == 0:
                prepare(*stage)
    for out in DEPARTURES:
        leave(out)


def on_device(dims, views, weights):
    n, nz = dims
    _, rows, feats = views.shape
    _, own_rows, width = weights.shape
    _, count = arrivals(n)
    near, reach = nz // 2, nz // 4
    strip = nz * 2 * PIECE
    half, full, dma = jnp.bfloat16, jnp.float32, pltpu.SemaphoreType.DMA
    lead = (ITERS,)
    tile = (near, PIECE, HALF)
    scratch = [
        pltpu.VMEM((rows, feats), half),
        pltpu.VMEM((own_rows, width), full),
        pltpu.VMEM((2, 2, strip, strip), half),
        pltpu.VMEM((2, 2, rows, feats // 4), half),
        pltpu.VMEM((2, 2, n, n, near * PIECE, rows), half),
        pltpu.VMEM(lead + (2, 2, n, n, near, PIECE, width), half),
        pltpu.VMEM(lead + (rows, width), full),
        pltpu.VMEM(lead + (rows, width), full),
        pltpu.VMEM((rows, width), half),
        pltpu.VMEM(lead + (n * n, 1, width), full),
        pltpu.VMEM(lead + (2 * nz, 1, width), full),
        pltpu.VMEM(lead + (3, 2, n, n) + tile, half),
        pltpu.VMEM(lead + (2, n, n) + tile, half),
        pltpu.VMEM(lead + (n, 2, 2, n, reach, PIECE, HALF), half),
        pltpu.VMEM(lead + (3, n, 2, n - 1) + tile, half),
        pltpu.VMEM(lead + (3, 2, n - 1) + tile, half),
        pltpu.VMEM(lead + (3, 2, n - 1) + tile, half),
        pltpu.VMEM(lead + (near, 2, PIECE, width), half),
        pltpu.VMEM(lead + (near, 2, PIECE, HALF), half),
        pltpu.VMEM(lead + (near, 2, PIECE, width), half),
        pltpu.VMEM(lead + (near, 2, PIECE, HALF), half),
        dma((len(DEPARTURES),)),
        dma((count,)),
        dma((2,)),
    ]
    total_rows = rows * n * n * nz
    vmem = pl.BlockSpec(memory_space=pltpu.VMEM)
    hbm = pl.BlockSpec(memory_space=pl.ANY)
    flops = 4 * ITERS * rows * feats * width
    new, shown = pl.pallas_call(
        functools.partial(kernel, dims, total_rows, math.sqrt(feats)),
        out_shape=(
            jax.ShapeDtypeStruct((own_rows, width), full),
            jax.ShapeDtypeStruct((rows, width), half),
        ),
        in_specs=[hbm, hbm],
        out_specs=(vmem, vmem),
        scratch_shapes=scratch,
        compiler_params=pltpu.CompilerParams(
            collective_id=0, has_side_effects=True, vmem_limit_bytes=56 << 20
        ),
        cost_estimate=pl.CostEstimate(flops=flops, bytes_accessed=2 * rows * feats, transcendentals=0),
        name="cca_steps",
    )(views[0], weights[0])
    return new[None], shown[None]


def solution(mesh):
    dims = (math.isqrt(mesh.shape["row"]), mesh.shape["feat"])
    spec = P("view", ("row", "feat"), None)
    return jax.shard_map(
        functools.partial(on_device, dims),
        mesh=mesh,
        in_specs=(spec, spec),
        out_specs=(spec, spec),
        check_vma=False,
    )
```
